32 devices in a mesh: dp: 16 (over z, x, core), group: 2 (over y).
Axes of the slice: x: 2, y: 2, z: 4, core: 2. Of those that a mesh axis runs over, the one named last changes fastest.
Arguments:
- tokens: bfloat16 [16384, 7168], P('dp', 'group'), may hold values from -6 to 6
- proj_in: bfloat16 [32, 1024, 2, 7168], P(None, 'dp', None, 'group'), may hold values from -0.0625 to 0.0625
- proj_out: bfloat16 [32, 1024, 7168], P(None, 'dp', 'group'), may hold values from -0.1875 to 0.1875
- expert_list: int32 [16, 2], replicated, may hold values from 0 to 31, as said below
- block_pattern: int32 [16, 2, 8], replicated, may hold values from 0 to 1, as said below
- route_weight: float32 [16384, 2], P('dp'), may hold values from 0.1 to 1
Outputs:
- mixed: bfloat16 [16384, 7168], P('dp', 'group')
The draws below stay inside these ranges and needn't reach their ends.
Inputs may be any that keep to these rules, and one draw needn't show every extreme that they name: `expert_list`: each row names 2 different experts of the window. `block_pattern`: 1 where the list slot's expert acts on that block of 128 tokens, else 0; the share of ones differs from token group to token group, and in every draw some token group has every block of every slot set.
All inputs are finite; a program needn't handle non-finite values.
Results may differ from the reference program's by a relative error of at most 0.025.
Values may be sent and summed in bfloat16 or wider, within the bound.
No kernel may reach another device: no remote copies, remote signals or barrier semaphores. Data moves between devices by JAX's collectives and lax.ppermute only.
A program may use at most 256 MiB of HBM per device.

```python
import math
import jax
import jax.numpy as jnp
from jax import lax

D = 7168
FF = 1024
EXPERTS = 32
LIST = 2
BLOCK = 128
TOK_DEV = 1024
NBLK = 8
TOKENS = 16384
N_DP = 16
N_GROUP = 2


def draw_expert_list(key, part):
    row_keys = jax.random.split(jax.random.fold_in(key, 11), N_DP)
    chosen = jax.vmap(lambda one_key: jax.random.permutation(one_key, EXPERTS)[:LIST])(row_keys)
    return chosen.astype(jnp.int32)


def draw_block_pattern(key, part):
    key_level = jax.random.fold_in(key, 21)
    key_bits = jax.random.fold_in(key, 22)
    key_busy = jax.random.fold_in(key, 23)
    fill_level = jax.random.randint(key_level, (N_DP, 1, 1), 1, 9)
    busiest = jax.random.randint(key_busy, (), 0, N_DP)
    row_index = jnp.arange(N_DP, dtype=jnp.int32)[:, None, None]
    fill_level = jnp.where(row_index == busiest, 8, fill_level)
    random_bits = jax.random.randint(key_bits, (N_DP, LIST, NBLK), 0, 8)
    return (random_bits < fill_level).astype(jnp.int32)


def levels(rng, extent, pieces, low, largest):
    factor_of, own = 1.0, jax.random.fold_in(rng, 6)
    for dim, shards_of in pieces:
        heights = jnp.exp(jax.random.uniform(jax.random.fold_in(own, dim), (shards_of,), jnp.float32, low / len(pieces), largest / len(pieces)))
        factor_of = factor_of * jnp.repeat(heights, extent[dim] // shards_of).reshape([-1 if axis == dim else 1 for axis in range(len(extent))])
    return factor_of


def centred(rng, shape, spread, reach, shards=(), kind=jnp.bfloat16):
    result = jax.random.normal(rng, shape, jnp.float32) * spread
    if len(shards) > 0:
        result = levels(rng, shape, shards, -0.22, 0.18) * result
    return jnp.clip(result, min=-reach, max=reach).astype(kind)


def setup_inputs(seed: int = 0) -> dict:
    splits = jax.random.split(jax.random.key(seed), 7)
    return {
        "tokens": centred(splits[0], (TOKENS, D), 1.0, 6.0, ((0, 16), (1, 2))),
        "proj_in": centred(splits[1], (EXPERTS, FF, 2, D), D ** -0.5, 0.0625, ((1, 16), (3, 2))),
        "proj_out": centred(splits[2], (EXPERTS, FF, D), FF ** -0.5, 0.1875, ((1, 16), (2, 2))),
        "expert_list": draw_expert_list(jax.random.fold_in(splits[6], 71), 0),
        "block_pattern": draw_block_pattern(jax.random.fold_in(splits[6], 71), 0),
        "route_weight": jnp.clip(jnp.exp(math.log(1.0) - 2.3025851 * jax.random.uniform(splits[5], (TOKENS, LIST), jnp.float32) ** levels(splits[5], (TOKENS, LIST), ((0, 16),), -0.2, 0.2)), 0.1, 1.0),
    }


def reference(tokens, proj_in, proj_out, expert_list, block_pattern, route_weight):
    group_width = D // N_GROUP
    group_rows = tokens.reshape(N_DP, TOK_DEV, D)
    group_weights = route_weight.reshape(N_DP, TOK_DEV, LIST)

    def one_group(inputs):
        token_rows, listed, pattern, weights_here = inputs
        block_mask = jnp.repeat(pattern, BLOCK, axis=1).astype(jnp.float32)
        combined = jnp.zeros((TOK_DEV, D), jnp.float32)
        for list_slot in range(LIST):
            expert = listed[list_slot].astype(jnp.int32)
            weight_in = lax.dynamic_index_in_dim(proj_in, expert, 0, keepdims=False)
            weight_out = lax.dynamic_index_in_dim(proj_out, expert, 0, keepdims=False)
            gate_up = jnp.zeros((TOK_DEV, FF * 2), jnp.float32)
            for column_part in range(N_GROUP):
                low = column_part * group_width
                token_cols = token_rows[:, low:low + group_width]
                weight_cols = weight_in[:, :, low:low + group_width].reshape(FF * 2, group_width)
                partial_value = jnp.dot(token_cols, weight_cols.T, preferred_element_type=jnp.float32)
                rounded = lax.optimization_barrier(partial_value.astype(jnp.bfloat16))
                gate_up = gate_up + rounded.astype(jnp.float32)
            gate_up = gate_up.reshape(TOK_DEV, FF, 2)
            token_scale = weights_here[:, list_slot] * block_mask[list_slot]
            hidden = (token_scale[:, None] * jax.nn.silu(gate_up[:, :, 0]) * gate_up[:, :, 1]).astype(jnp.bfloat16)
            combined = combined + jnp.dot(hidden, weight_out, preferred_element_type=jnp.float32)
        return combined.astype(jnp.bfloat16)

    mixed = lax.map(one_group, (group_rows, expert_list, block_pattern, group_weights))
    return mixed.reshape(TOKENS, D)
```

```python
import jax
import jax.numpy as jnp
from jax import lax
from jax.sharding import PartitionSpec as P

SLABS = 4
CHUNKS = 4


def on_device(tokens, proj_in, proj_out, expert_list, block_pattern, route_weight):
    dp_size = lax.axis_size("dp")
    group_size = lax.axis_size("group")
    peers = dp_size // SLABS
    dp_index = lax.axis_index("dp")
    slab = dp_index // peers
    column = dp_index % peers
    rows, width = tokens.shape
    slots = expert_list.shape[1]
    blocks = block_pattern.shape[2]
    units = proj_in.shape[1]
    step = rows // CHUNKS

    def over_z(value, hops):
        pairs = [(a * peers + j, b * peers + j) for a, b in hops for j in range(peers)]
        return lax.ppermute(value, "dp", pairs)

    def over_peers(value, offset):
        pairs = [
            (a * peers + j, a * peers + (j + offset) % peers)
            for a in range(SLABS)
            for j in range(peers)
        ]
        return lax.ppermute(value, "dp", pairs)

    swap_half = [(0, 1), (1, 0), (2, 3), (3, 2)]
    middle = [(1, 2), (2, 1)]
    outward = [(1, 0), (2, 3)]
    inward = [(0, 1), (3, 2)]
    low_half = slab < 2
    outer = (slab == 0) | (slab == 3)
    slab_of = [
        jnp.where(low_half, 3, 0),
        jnp.where(low_half, 2, 1),
        slab ^ 1,
        slab,
    ]

    scale_all = lax.all_gather(route_weight.T, "dp", axis=0)
    mask_all = jnp.repeat(block_pattern, rows // blocks, axis=2).astype(jnp.float32)

    def scale_of(turn):
        group = slab_of[turn] * peers + column
        return lax.dynamic_index_in_dim(scale_all, group, 0, keepdims=False) * (
            lax.dynamic_index_in_dim(mask_all, group, 0, keepdims=False)
        )

    def weights_of(turn):
        got_in, got_out = [], []
        for offset in range(peers):
            group = slab_of[turn] * peers + (column + offset) % peers
            chosen = lax.dynamic_index_in_dim(expert_list, group, 0, keepdims=False)
            part_in = jnp.stack(
                [lax.dynamic_index_in_dim(proj_in, chosen[l], 0, keepdims=False) for l in range(slots)]
            )
            part_out = jnp.stack(
                [lax.dynamic_index_in_dim(proj_out, chosen[l], 0, keepdims=False) for l in range(slots)]
            )
            if offset:
                part_in = over_peers(part_in, offset)
                part_out = over_peers(part_out, offset)
            got_in.append(part_in)
            got_out.append(part_out)
        return jnp.concatenate(got_in, axis=1), jnp.concatenate(got_out, axis=1)

    def hidden_of(token_rows, weight_in, scale):
        part = jnp.einsum(
            "td,lfcd->lctf", token_rows, weight_in, preferred_element_type=jnp.float32
        ).astype(jnp.bfloat16)
        total = part.astype(jnp.float32)
        for offset in range(1, group_size):
            pairs = [(i, (i + offset) % group_size) for i in range(group_size)]
            total = total + lax.ppermute(part, "group", pairs).astype(jnp.float32)
        return (scale[:, :, None] * jax.nn.silu(total[:, 0]) * total[:, 1]).astype(jnp.bfloat16)

    def out_of(hidden, weight_out):
        return jnp.einsum("ltf,lfd->td", hidden, weight_out, preferred_element_type=jnp.float32)

    weights = [weights_of(turn) for turn in range(4)]
    scales = [scale_of(turn) for turn in range(4)]
    results = []
    for chunk in range(CHUNKS):
        low = chunk * step
        own = tokens[low : low + step]
        near = over_z(own, swap_half)
        inner = over_z(own, middle)
        far_mid = over_z(near, middle)
        far = jnp.where(outer, over_z(far_mid, outward), far_mid)
        inner = jnp.where(outer, over_z(inner, outward), inner)
        partial = []
        for turn, token_rows in enumerate((far, inner, near, own)):
            hidden = hidden_of(token_rows, weights[turn][0], scales[turn][:, low : low + step])
            partial.append(out_of(hidden, weights[turn][1]))

        def send(value, hops):
            return over_z(value.astype(jnp.bfloat16), hops).astype(jnp.float32)

        to_far = partial[0] + send(partial[0], inward)
        to_inner = partial[1] + send(partial[1], inward)
        to_near = partial[2] + send(to_far, middle)
        own_sum = partial[3] + send(to_inner, middle) + send(to_near, swap_half)
        results.append(own_sum.astype(jnp.bfloat16))
    return jnp.concatenate(results, axis=0)


def solution(mesh):
    return jax.shard_map(
        on_device,
        mesh=mesh,
        in_specs=(
            P("dp", "group"),
            P(None, "dp", None, "group"),
            P(None, "dp", "group"),
            P(),
            P(),
            P("dp", None),
        ),
        out_specs=P("dp", "group"),
        check_vma=False,
    )
```

```python
import jax
import jax.numpy as jnp
from jax import lax
from jax.experimental import pallas as pl
from jax.experimental.pallas import tpu as pltpu
from jax.sharding import PartitionSpec as P

SLABS = 4


def gather_kernel(chosen, source, *rest):
    count = chosen.shape[0]
    paired = len(source.shape) == 4
    if paired:
        outs, held, flat, sems = rest[:-3], rest[-3], rest[-2], rest[-1]
    else:
        outs, held, sems = rest[:-2], rest[-2], rest[-1]
        flat = held
    slots = count // len(outs)
    units = flat.shape[1]
    moves = []
    for n in range(count):
        k, l = divmod(n, slots)
        moves.append(
            (
                pltpu.make_async_copy(source.at[chosen[n]], held.at[n], sems.at[0, n]),
                pltpu.make_async_copy(
                    flat.at[n], outs[k].at[pl.ds(l * units, units)], sems.at[1, n]
                ),
            )
        )
    for into, _ in moves:
        into.start()
    for n, (into, out) in enumerate(moves):
        into.wait()
        if paired:

            @pl.loop(0, units // 16)
            def _(block):
                pairs = held[n, pl.ds(block * 8, 8)]
                flat[n, pl.ds(pl.multiple_of(block * 16, 16), 16)] = pairs.reshape(16, flat.shape[2])

        out.start()
    for _, out in moves:
        out.wait()


def gather_experts(chosen, source, parts):
    count = chosen.shape[0]
    width = source.shape[-1]
    units = source.size // (source.shape[0] * width)
    scratch = [pltpu.VMEM((count,) + source.shape[1:], source.dtype)]
    if source.ndim == 4:
        scratch.append(pltpu.VMEM((count, units, width), source.dtype))
    return pl.pallas_call(
        gather_kernel,
        out_shape=[jax.ShapeDtypeStruct((count // parts * units, width), source.dtype)] * parts,
        grid_spec=pltpu.PrefetchScalarGridSpec(
            num_scalar_prefetch=1,
            grid=(),
            in_specs=[pl.BlockSpec(memory_space=pl.ANY)],
            out_specs=[pl.BlockSpec(memory_space=pl.ANY)] * parts,
            scratch_shapes=scratch + [pltpu.SemaphoreType.DMA((2, count))],
        ),
        compiler_params=pltpu.CompilerParams(vmem_limit_bytes=40 << 20),
    )(chosen, source)


def hold_kernel(*refs):
    del refs


def hold_until(values, landed):
    count = len(values)
    anywhere = pl.BlockSpec(memory_space=pl.ANY)
    return pl.pallas_call(
        hold_kernel,
        out_shape=[jax.ShapeDtypeStruct(v.shape, v.dtype) for v in values],
        in_specs=[anywhere] * (count + len(landed)),
        out_specs=[anywhere] * count,
        input_output_aliases={n: n for n in range(count)},
        compiler_params=pltpu.CompilerParams(vmem_limit_bytes=1 << 20),
    )(*values, *landed)


def on_device(tokens, proj_in, proj_out, expert_list, block_pattern, route_weight):
    dp_size = lax.axis_size("dp")
    group_size = lax.axis_size("group")
    peers = dp_size // SLABS
    dp_index = lax.axis_index("dp")
    slab = dp_index // peers
    column = dp_index % peers
    rows, width = tokens.shape
    slots = expert_list.shape[1]
    units = proj_in.shape[1]
    block_rows = rows // block_pattern.shape[2]

    def over_z(value, hops, offset=0):
        pairs = [(a * peers + j, b * peers + (j ^ offset)) for a, b in hops for j in range(peers)]
        return lax.ppermute(value, "dp", pairs)

    rightward = [(0, 1), (1, 2), (2, 3)]
    leftward = [(3, 2), (2, 1), (1, 0)]
    middle = [(1, 2), (2, 1)]
    low_half = slab < 2
    outer = (slab == 0) | (slab == 3)
    far, mid, near, own = 0, 1, 2, 3
    slab_of = [jnp.where(low_half, 3, 0), jnp.where(low_half, 2, 1), slab ^ 1, slab]

    def gather(source, slabs):
        chosen = jnp.concatenate(
            [
                lax.dynamic_index_in_dim(expert_list, s * peers + (column ^ o), 0, keepdims=False)
                for o in range(peers)
                for s in slabs
            ]
        )
        return gather_experts(chosen, source, peers)

    def over_peers(parts, name):
        same = [(a, a) for a in range(SLABS)]
        with jax.named_scope("hop_" + name):
            return [parts[0]] + [over_z(parts[o], same, o) for o in range(1, peers)]

    def joined(parts, place, places):
        size = parts[0].shape[0] // places
        return jnp.concatenate([part[place * size : (place + 1) * size] for part in parts], axis=0)

    def held(parts, landed):
        return [parts[0]] + list(hold_until(parts[1:], landed))

    first = gather(proj_in, [slab_of[far], slab_of[near]])
    with jax.named_scope("hop_right1"):
        right1 = over_z(tokens, rightward)
    with jax.named_scope("hop_left1"):
        left1 = over_z(tokens, leftward)
    first = over_peers(first, "in_far_near")
    far_in, near_in = joined(first, 0, 2), joined(first, 1, 2)

    with jax.named_scope("hop_right2"):
        right2 = over_z(right1, [(1, 2), (2, 3)])
    with jax.named_scope("hop_left2"):
        left2 = over_z(left1, [(2, 1), (1, 0)])
    with jax.named_scope("hop_edge"):
        edge_in = over_z(far_in, [(0, 1), (3, 2)])
    second = over_peers(
        held(gather(proj_out, [slab ^ 2, slab ^ 3]), first[1:] + [right1, left1]), "out23"
    )
    out2, out3 = joined(second, 0, 2), joined(second, 1, 2)

    def terms_of(token_rows, weight_in):
        return lax.dot_general(
            weight_in, token_rows, (((1,), (1,)), ((), ())), preferred_element_type=jnp.float32
        ).astype(jnp.bfloat16)

    def hidden_of(name, part):
        total = part.astype(jnp.float32)
        for offset in range(1, group_size):
            pairs = [(g, (g + offset) % group_size) for g in range(group_size)]
            with jax.named_scope("terms_" + name):
                total = total + lax.ppermute(part, "group", pairs).astype(jnp.float32)
        total = total.reshape(-1, 2, rows)
        return (jax.nn.silu(total[:, 0]) * total[:, 1]).astype(jnp.bfloat16)

    toward1 = jnp.where(low_half, left1, right1)
    away1 = jnp.where(low_half, right1, left1)
    near_hidden = hidden_of("near", terms_of(jnp.where(outer, toward1, away1), near_in))
    with jax.named_scope("hop_hidden1"):
        hidden1 = over_z(near_hidden, [(a, a ^ 1) for a in range(SLABS)])

    out2, out3 = hold_until([out2, out3], [right2, left2, hidden1])
    with jax.named_scope("hop_out2"):
        out2 = over_z(out2, [(a, a ^ 2) for a in range(SLABS)])
    with jax.named_scope("hop_out3"):
        out3 = over_z(out3, [(a, a ^ 3) for a in range(SLABS)])
    third = over_peers(
        held(gather(proj_in, [slab_of[mid]]), second[1:] + [right2, left2, hidden1]), "in_mid"
    )
    mid_in = joined(third, 0, 1)

    toward2 = jnp.where(low_half, left2, right2)
    far_hidden = hidden_of("far", terms_of(toward2, far_in))
    edge_hidden = hidden_of("edge", terms_of(toward2, edge_in))
    mid_hidden = hidden_of("mid", terms_of(jnp.where(outer, toward2, toward1), mid_in))

    fourth = over_peers(held(gather(proj_out, [slab, slab ^ 1]), third[1:]), "out01")
    out0, out1 = joined(fourth, 0, 2), joined(fourth, 1, 2)
    with jax.named_scope("hop_out1"):
        out1 = over_z(out1, [(a, a ^ 1) for a in range(SLABS)])
    fifth = over_peers(held(gather(proj_in, [slab]), fourth[1:]), "in_own")
    own_hidden = hidden_of("own", terms_of(tokens, joined(fifth, 0, 1)))

    cross_hidden = jnp.where(outer, mid_hidden, far_hidden)
    cross_hidden, edge_hidden, mid_hidden = hold_until(
        [cross_hidden, edge_hidden, mid_hidden], [out2, out3]
    )
    with jax.named_scope("hop_hidden2"):
        hidden2 = over_z(cross_hidden, [(a, a ^ 2) for a in range(SLABS)])
    with jax.named_scope("hop_hidden3"):
        hidden3 = jnp.where(
            outer, over_z(edge_hidden, [(1, 3), (2, 0)]), over_z(mid_hidden, middle)
        )

    own_pattern = lax.dynamic_index_in_dim(block_pattern, dp_index, 0, keepdims=False)
    scale = route_weight.T * jnp.repeat(own_pattern, block_rows, axis=1).astype(jnp.float32)

    def weighted(hidden):
        split = hidden.astype(jnp.float32).reshape(peers, slots, units, rows)
        return (split * scale[None, :, None, :]).astype(jnp.bfloat16).reshape(-1, rows)

    total = 0.0
    for hidden, weight_out in ((own_hidden, out0), (hidden1, out1), (hidden2, out2), (hidden3, out3)):
        total = total + lax.dot_general(
            weighted(hidden),
            weight_out,
            (((0,), (0,)), ((), ())),
            preferred_element_type=jnp.float32,
        )
    return total.astype(jnp.bfloat16)


def solution(mesh):
    return jax.shard_map(
        on_device,
        mesh=mesh,
        in_specs=(
            P("dp", "group"),
            P(None, "dp", None, "group"),
            P(None, "dp", "group"),
            P(),
            P(),
            P("dp", None),
        ),
        out_specs=P("dp", "group"),
        check_vma=False,
    )
```

```python
import functools

import jax
import jax.numpy as jnp
from jax import lax
from jax.experimental import pallas as pl
from jax.experimental.pallas import tpu as pltpu
from jax.sharding import PartitionSpec as P

SLABS = 4
CORES = 2


def gather_kernel(counts, chosen, proj_in, proj_out, *rest):
    outs, (held_in, flat_in, held_out, sems) = rest[:-4], rest[-4:]
    count_in, count_out = counts
    high_in, high_out = flat_in.shape[1], held_out.shape[1]
    size = count_in * high_in + count_out * high_out
    moves = []
    for core in range(CORES):
        out, base = (outs[0], core * size) if len(outs) == 1 else (outs[core], 0)
        for n in range(count_in + count_out):
            item = core * (count_in + count_out) + n
            if n < count_in:
                slot, row = core * count_in + n, base + n * high_in
                into = pltpu.make_async_copy(
                    proj_in.at[chosen[item]], held_in.at[slot], sems.at[0, item]
                )
                move = pltpu.make_async_copy(
                    flat_in.at[slot], out.at[pl.ds(row, high_in)], sems.at[1, item]
                )
            else:
                slot = core * count_out + n - count_in
                row = base + count_in * high_in + (n - count_in) * high_out
                into = pltpu.make_async_copy(
                    proj_out.at[chosen[item]], held_out.at[slot], sems.at[0, item]
                )
                move = pltpu.make_async_copy(
                    held_out.at[slot], out.at[pl.ds(row, high_out)], sems.at[1, item]
                )
            moves.append((into, move, slot if n < count_in else None))
    for into, _, _ in moves:
        into.start()
    for into, move, slot in moves:
        into.wait()
        if slot is not None:

            @pl.loop(0, high_in // 16)
            def _(block):
                pairs = held_in[slot, pl.ds(block * 8, 8)]
                flat_in[slot, pl.ds(pl.multiple_of(block * 16, 16), 16)] = pairs.reshape(
                    16, flat_in.shape[2]
                )

        move.start()
    for _, move, _ in moves:
        move.wait()


def gather_experts(chosen, proj_in, proj_out, counts, parts):
    width = proj_in.shape[-1]
    high_in, high_out = 2 * proj_in.shape[1], proj_out.shape[1]
    rows = CORES * (counts[0] * high_in + counts[1] * high_out)
    anywhere = pl.BlockSpec(memory_space=pl.ANY)
    got = pl.pallas_call(
        functools.partial(gather_kernel, counts),
        out_shape=[jax.ShapeDtypeStruct((rows // parts, width), proj_in.dtype)] * parts,
        grid_spec=pltpu.PrefetchScalarGridSpec(
            num_scalar_prefetch=1,
            grid=(),
            in_specs=[anywhere] * 2,
            out_specs=[anywhere] * parts,
            scratch_shapes=[
                pltpu.VMEM((max(CORES * counts[0], 1),) + proj_in.shape[1:], proj_in.dtype),
                pltpu.VMEM((max(CORES * counts[0], 1), high_in, width), proj_in.dtype),
                pltpu.VMEM((max(CORES * counts[1], 1), high_out, width), proj_out.dtype),
                pltpu.SemaphoreType.DMA((2, CORES * sum(counts))),
            ],
        ),
        compiler_params=pltpu.CompilerParams(vmem_limit_bytes=40 << 20),
    )(chosen, proj_in, proj_out)
    return list(got)


def hold_kernel(*refs):
    del refs


def hold_until(values, landed):
    count = len(values)
    anywhere = pl.BlockSpec(memory_space=pl.ANY)
    return pl.pallas_call(
        hold_kernel,
        out_shape=[jax.ShapeDtypeStruct(v.shape, v.dtype) for v in values],
        in_specs=[anywhere] * (count + len(landed)),
        out_specs=[anywhere] * count,
        input_output_aliases={n: n for n in range(count)},
        compiler_params=pltpu.CompilerParams(vmem_limit_bytes=1 << 20),
    )(*values, *landed)


def add_product_kernel(left, right, total, result):
    product = jnp.dot(left[...], right[...], preferred_element_type=jnp.float32)
    result[...] = (total[...] + product).astype(result.dtype)


def add_product(left, right, total):
    rows, depth = left.shape
    width = right.shape[1]
    block = next(n for n in (512, 384, 256, 128) if width % n == 0)
    return pl.pallas_call(
        add_product_kernel,
        grid=(width // block,),
        in_specs=[
            pl.BlockSpec((rows, depth), lambda n: (0, 0)),
            pl.BlockSpec((depth, block), lambda n: (0, n)),
            pl.BlockSpec((rows, block), lambda n: (0, n)),
        ],
        out_specs=pl.BlockSpec((rows, block), lambda n: (0, n)),
        out_shape=jax.ShapeDtypeStruct((rows, width), left.dtype),
        compiler_params=pltpu.CompilerParams(vmem_limit_bytes=24 << 20),
    )(left, right, total)


def on_device(tokens, proj_in, proj_out, expert_list, block_pattern, route_weight):
    dp_size = lax.axis_size("dp")
    group_size = lax.axis_size("group")
    peers = dp_size // SLABS
    dp_index = lax.axis_index("dp")
    group_index = lax.axis_index("group")
    slab = dp_index // peers
    column = dp_index % peers
    rows = tokens.shape[0]
    slots = expert_list.shape[1]
    units = proj_in.shape[1]
    block_rows = rows // block_pattern.shape[2]
    share = rows // group_size

    def over_z(value, hops, offset=0):
        pairs = [(a * peers + j, b * peers + (j ^ offset)) for a, b in hops for j in range(peers)]
        return lax.ppermute(value, "dp", pairs)

    def over_group(value, offset):
        pairs = [(g, (g + offset) % group_size) for g in range(group_size)]
        return lax.ppermute(value, "group", pairs)

    same = [(a, a) for a in range(SLABS)]
    middle = [(1, 2), (2, 1)]
    low_half = slab < 2
    outer = (slab == 0) | (slab == 3)
    far, mid, near, own = jnp.where(low_half, 3, 0), jnp.where(low_half, 2, 1), slab ^ 1, slab

    def gathered(in_slabs, out_slabs):
        counts = (slots * len(in_slabs), slots * len(out_slabs))

        def slices(chip, parts):
            chosen = jnp.concatenate(
                [
                    lax.dynamic_index_in_dim(
                        expert_list, s * peers + (column ^ (CORES * chip + core)), 0, keepdims=False
                    )
                    for core in range(CORES)
                    for s in in_slabs + out_slabs
                ]
            )
            return gather_experts(chosen, proj_in, proj_out, counts, parts)

        kept, sibling = slices(0, CORES)
        return [slices(chip, 1)[0] for chip in range(1, peers // CORES)] + [kept, sibling]

    def over_chips(name, gather, start_after):
        sends = gather[:-2]
        if start_after:
            sends = hold_until(sends, start_after)
        with jax.named_scope("hop_chips_" + name):
            return [over_z(v, same, CORES * (n + 1)) for n, v in enumerate(sends)]

    def over_cores(name, gather, across, merged=True):
        kept, sibling = gather[-2:]
        size = kept.shape[0]
        parts = [sibling] + [v[size:] for v in across]
        if merged:
            parts = [jnp.concatenate(parts, axis=0)]
        else:
            parts[:1] = hold_until(parts[:1], across)
        with jax.named_scope("hop_cores_" + name):
            swapped = [over_z(v, same, 1) for v in parts]
        if merged:
            swapped = [swapped[0][n * size : (n + 1) * size] for n in range(1 + len(across))]
        return [kept] + [v[:size] for v in across] + swapped

    def joined(pieces, low, high):
        return jnp.concatenate([v[low:high] for v in pieces], axis=0)

    rows_in, rows_out = slots * units * 2, slots * units

    def terms_of(token_rows, weight_in):
        return lax.dot_general(
            weight_in, token_rows, (((1,), (1,)), ((), ())), preferred_element_type=jnp.float32
        ).astype(jnp.bfloat16)

    def gated(total):
        total = total.reshape(-1, 2, total.shape[1])
        return (jax.nn.silu(total[:, 0]) * total[:, 1]).astype(jnp.bfloat16)

    def hidden_of(name, part):
        total = part.astype(jnp.float32)
        for offset in range(1, group_size):
            with jax.named_scope("terms_" + name):
                total = total + over_group(part, offset).astype(jnp.float32)
        return gated(total)

    def hidden_share_of(name, part):
        def share_of(member):
            return lax.dynamic_slice_in_dim(part, member * share, share, 1)

        total = share_of(group_index).astype(jnp.float32)
        for offset in range(1, group_size):
            with jax.named_scope("terms_" + name):
                moved = over_group(share_of((group_index + offset) % group_size), offset)
                total = total + moved.astype(jnp.float32)
        return gated(total)

    def all_rows(name, piece):
        result = jnp.zeros((piece.shape[0], rows), piece.dtype)
        for offset in range(group_size):
            with jax.named_scope("terms_" + name):
                moved = over_group(piece, offset) if offset else piece
            member = (group_index - offset) % group_size
            result = lax.dynamic_update_slice_in_dim(result, moved, member * share, 1)
        return result

    first = gathered([far], [slab ^ 2, slab ^ 3])
    second = gathered([mid, near], [])
    third = gathered([own], [own, near])

    with jax.named_scope("hop_right1"):
        right1 = over_z(tokens, [(0, 1), (1, 2), (2, 3)])
    with jax.named_scope("hop_left1"):
        left1 = over_z(tokens, [(3, 2), (2, 1), (1, 0)])
    across1 = over_chips("one", first, [])
    across1 = list(hold_until(across1, [right1, left1] + second + third))

    with jax.named_scope("hop_right2"):
        right2 = over_z(right1, [(1, 2), (2, 3)])
    with jax.named_scope("hop_left2"):
        left2 = over_z(left1, [(2, 1), (1, 0)])
    across2 = over_chips("two", second, across1)
    pieces = over_cores("one", first, across1, merged=False)
    far_in = joined(pieces, 0, rows_in)
    out2 = joined(pieces, rows_in, rows_in + rows_out)
    out3 = joined(pieces, rows_in + rows_out, rows_in + 2 * rows_out)
    with jax.named_scope("hop_edge"):
        edge_in = over_z(far_in, [(0, 1), (3, 2)])

    (out2,) = hold_until([out2], [right2, left2] + across2)
    with jax.named_scope("hop_out2"):
        out2 = over_z(out2, [(a, a ^ 2) for a in range(SLABS)])
    across3 = over_chips("three", third, across2 + [right2, left2])
    pieces = over_cores("two", second, across2)
    mid_in, near_in = joined(pieces, 0, rows_in), joined(pieces, rows_in, 2 * rows_in)
    toward1 = jnp.where(low_half, left1, right1)
    away1 = jnp.where(low_half, right1, left1)
    toward2 = jnp.where(low_half, left2, right2)
    far_hidden = hidden_share_of("far", terms_of(toward2, far_in))
    mid_hidden = hidden_share_of("mid", terms_of(jnp.where(outer, toward2, toward1), mid_in))
    edge_hidden = hidden_share_of("edge", terms_of(toward2, edge_in))
    near_hidden = hidden_of("near", terms_of(jnp.where(outer, toward1, away1), near_in))
    cross_hidden = jnp.where(outer, mid_hidden, far_hidden)
    with jax.named_scope("hop_hidden3"):
        edge_hidden = over_z(edge_hidden, [(1, 3), (2, 0)])

    out3, cross_hidden, mid_hidden = hold_until(
        [out3, cross_hidden, mid_hidden], [out2, near_hidden, edge_hidden]
    )
    across3 = list(hold_until(across3, [out3, cross_hidden, mid_hidden]))
    with jax.named_scope("hop_out3"):
        out3 = over_z(out3, [(a, a ^ 3) for a in range(SLABS)])
    with jax.named_scope("hop_hidden2"):
        hidden2 = over_z(cross_hidden, [(a, a ^ 2) for a in range(SLABS)])
    with jax.named_scope("hop_hidden3"):
        hidden3 = jnp.where(outer, edge_hidden, over_z(mid_hidden, middle))
    pieces = over_cores("three", third, across3)
    own_in = joined(pieces, 0, rows_in)
    out0 = joined(pieces, rows_in, rows_in + rows_out)
    out1 = joined(pieces, rows_in + rows_out, rows_in + 2 * rows_out)
    both1 = jnp.concatenate([out1, near_hidden], axis=1)
    with jax.named_scope("hop_out1"):
        both1 = over_z(both1, [(a, a ^ 1) for a in range(SLABS)])
    out1, hidden1 = both1[:, : out1.shape[1]], both1[:, out1.shape[1] :]
    own_hidden = hidden_of("own", terms_of(tokens, own_in))

    own_pattern = lax.dynamic_index_in_dim(block_pattern, dp_index, 0, keepdims=False)
    scale = route_weight.T * jnp.repeat(own_pattern, block_rows, axis=1).astype(jnp.float32)

    def weighted(hiddens):
        hidden = jnp.concatenate(hiddens, axis=0).astype(jnp.float32)
        hidden = hidden.reshape(-1, slots, units, rows) * scale[None, :, None, :]
        return hidden.astype(jnp.bfloat16).reshape(-1, rows)

    total = lax.dot_general(
        weighted([own_hidden, hidden1]),
        jnp.concatenate([out0, out1], axis=0),
        (((0,), (0,)), ((), ())),
        preferred_element_type=jnp.float32,
    )

    crossed = jnp.concatenate([hidden2, hidden3], axis=0)
    (crossed,) = hold_until([crossed], [out3, own_hidden])
    crossed = weighted([all_rows("rows", crossed)]).T
    return add_product(crossed, jnp.concatenate([out2, out3], axis=0), total)


def solution(mesh):
    return jax.shard_map(
        on_device,
        mesh=mesh,
        in_specs=(
            P("dp", "group"),
            P(None, "dp", None, "group"),
            P(None, "dp", "group"),
            P(),
            P(),
            P("dp", None),
        ),
        out_specs=P("dp", "group"),
        check_vma=False,
    )
```

```python
import functools

import jax
import jax.numpy as jnp
from jax import lax
from jax.experimental import pallas as pl
from jax.experimental.pallas import tpu as pltpu
from jax.sharding import PartitionSpec as P

SLABS = 4
CORES = 2


def gather_kernel(counts, chosen, proj_in, proj_out, *rest):
    outs, (held_in, flat_in, held_out, sems) = rest[:-4], rest[-4:]
    count_in, count_out = counts
    high_in, high_out = flat_in.shape[1], held_out.shape[1]
    size = count_in * high_in + count_out * high_out
    moves = []
    for core in range(CORES):
        out, base = (outs[0], core * size) if len(outs) == 1 else (outs[core], 0)
        for n in range(count_in + count_out):
            item = core * (count_in + count_out) + n
            if n < count_in:
                slot, row = core * count_in + n, base + n * high_in
                into = pltpu.make_async_copy(
                    proj_in.at[chosen[item]], held_in.at[slot], sems.at[0, item]
                )
                move = pltpu.make_async_copy(
                    flat_in.at[slot], out.at[pl.ds(row, high_in)], sems.at[1, item]
                )
            else:
                slot = core * count_out + n - count_in
                row = base + count_in * high_in + (n - count_in) * high_out
                into = pltpu.make_async_copy(
                    proj_out.at[chosen[item]], held_out.at[slot], sems.at[0, item]
                )
                move = pltpu.make_async_copy(
                    held_out.at[slot], out.at[pl.ds(row, high_out)], sems.at[1, item]
                )
            moves.append((into, move, slot if n < count_in else None))
    for into, _, _ in moves:
        into.start()
    for into, move, slot in moves:
        into.wait()
        if slot is not None:

            @pl.loop(0, high_in // 16)
            def _(block):
                pairs = held_in[slot, pl.ds(block * 8, 8)]
                flat_in[slot, pl.ds(pl.multiple_of(block * 16, 16), 16)] = pairs.reshape(
                    16, flat_in.shape[2]
                )

        move.start()
    for _, move, _ in moves:
        move.wait()


def gather_experts(chosen, proj_in, proj_out, counts, parts):
    width = proj_in.shape[-1]
    high_in, high_out = 2 * proj_in.shape[1], proj_out.shape[1]
    rows = CORES * (counts[0] * high_in + counts[1] * high_out)
    anywhere = pl.BlockSpec(memory_space=pl.ANY)
    got = pl.pallas_call(
        functools.partial(gather_kernel, counts),
        out_shape=[jax.ShapeDtypeStruct((rows // parts, width), proj_in.dtype)] * parts,
        grid_spec=pltpu.PrefetchScalarGridSpec(
            num_scalar_prefetch=1,
            grid=(),
            in_specs=[anywhere] * 2,
            out_specs=[anywhere] * parts,
            scratch_shapes=[
                pltpu.VMEM((max(CORES * counts[0], 1),) + proj_in.shape[1:], proj_in.dtype),
                pltpu.VMEM((max(CORES * counts[0], 1), high_in, width), proj_in.dtype),
                pltpu.VMEM((max(CORES * counts[1], 1), high_out, width), proj_out.dtype),
                pltpu.SemaphoreType.DMA((2, CORES * sum(counts))),
            ],
        ),
        compiler_params=pltpu.CompilerParams(vmem_limit_bytes=40 << 20),
    )(chosen, proj_in, proj_out)
    return list(got)


def hold_kernel(*refs):
    del refs


def hold_until(values, landed):
    count = len(values)
    anywhere = pl.BlockSpec(memory_space=pl.ANY)
    return pl.pallas_call(
        hold_kernel,
        out_shape=[jax.ShapeDtypeStruct(v.shape, v.dtype) for v in values],
        in_specs=[anywhere] * (count + len(landed)),
        out_specs=[anywhere] * count,
        input_output_aliases={n: n for n in range(count)},
        compiler_params=pltpu.CompilerParams(vmem_limit_bytes=1 << 20),
    )(*values, *landed)


def add_product_kernel(left, right_a, right_b, total, result):
    depth = right_a.shape[0]
    product = jnp.dot(left[:, :depth], right_a[...], preferred_element_type=jnp.float32)
    product += jnp.dot(left[:, depth:], right_b[...], preferred_element_type=jnp.float32)
    result[...] = (total[...] + product).astype(result.dtype)


def add_product(left, right_a, right_b, total):
    rows, depth = left.shape
    width = right_a.shape[1]
    block = next(n for n in (512, 384, 256, 128) if width % n == 0)
    return pl.pallas_call(
        add_product_kernel,
        grid=(width // block,),
        in_specs=[
            pl.BlockSpec((rows, depth), lambda n: (0, 0)),
            pl.BlockSpec((depth // 2, block), lambda n: (0, n)),
            pl.BlockSpec((depth // 2, block), lambda n: (0, n)),
            pl.BlockSpec((rows, block), lambda n: (0, n)),
        ],
        out_specs=pl.BlockSpec((rows, block), lambda n: (0, n)),
        out_shape=jax.ShapeDtypeStruct((rows, width), left.dtype),
        compiler_params=pltpu.CompilerParams(vmem_limit_bytes=24 << 20),
    )(left, right_a, right_b, total)


def on_device(tokens, proj_in, proj_out, expert_list, block_pattern, route_weight):
    dp_size = lax.axis_size("dp")
    group_size = lax.axis_size("group")
    peers = dp_size // SLABS
    dp_index = lax.axis_index("dp")
    group_index = lax.axis_index("group")
    slab = dp_index // peers
    column = dp_index % peers
    rows = tokens.shape[0]
    slots = expert_list.shape[1]
    units = proj_in.shape[1]
    block_rows = rows // block_pattern.shape[2]
    share = rows // group_size

    def over_z(value, hops, offset=0):
        pairs = [(a * peers + j, b * peers + (j ^ offset)) for a, b in hops for j in range(peers)]
        return lax.ppermute(value, "dp", pairs)

    def over_group(value, offset):
        pairs = [(g, (g + offset) % group_size) for g in range(group_size)]
        return lax.ppermute(value, "group", pairs)

    same = [(a, a) for a in range(SLABS)]
    middle = [(1, 2), (2, 1)]
    low_half = slab < 2
    outer = (slab == 0) | (slab == 3)
    far, mid, near, own = jnp.where(low_half, 3, 0), jnp.where(low_half, 2, 1), slab ^ 1, slab

    def gathered(in_slabs, out_slabs):
        counts = (slots * len(in_slabs), slots * len(out_slabs))

        def slices(chip, parts):
            chosen = jnp.concatenate(
                [
                    lax.dynamic_index_in_dim(
                        expert_list, s * peers + (column ^ (CORES * chip + core)), 0, keepdims=False
                    )
                    for core in range(CORES)
                    for s in in_slabs + out_slabs
                ]
            )
            return gather_experts(chosen, proj_in, proj_out, counts, parts)

        kept, sibling = slices(0, CORES)
        return [slices(chip, 1)[0] for chip in range(1, peers // CORES)] + [kept, sibling]

    def over_chips(name, gather, start_after):
        sends = gather[:-2]
        if start_after:
            sends = hold_until(sends, start_after)
        with jax.named_scope("hop_chips_" + name):
            return [over_z(v, same, CORES * (n + 1)) for n, v in enumerate(sends)]

    def over_cores(name, gather, across, merged=True):
        kept, sibling = gather[-2:]
        size = kept.shape[0]
        parts = [sibling] + [v[size:] for v in across]
        if merged:
            parts = [jnp.concatenate(parts, axis=0)]
        else:
            parts[:1] = hold_until(parts[:1], across)
        with jax.named_scope("hop_cores_" + name):
            swapped = [over_z(v, same, 1) for v in parts]
        if merged:
            swapped = [swapped[0][n * size : (n + 1) * size] for n in range(1 + len(across))]
        return [kept] + [v[:size] for v in across] + swapped

    def joined(pieces, low, high):
        return jnp.concatenate([v[low:high] for v in pieces], axis=0)

    rows_in, rows_out = slots * units * 2, slots * units

    def terms_of(token_rows, weight_in):
        return lax.dot_general(
            weight_in, token_rows, (((1,), (1,)), ((), ())), preferred_element_type=jnp.float32
        ).astype(jnp.bfloat16)

    def gated(total):
        total = total.reshape(-1, 2, total.shape[1])
        return (jax.nn.silu(total[:, 0]) * total[:, 1]).astype(jnp.bfloat16)

    def hidden_of(name, part):
        total = part.astype(jnp.float32)
        for offset in range(1, group_size):
            with jax.named_scope("terms_" + name):
                total = total + over_group(part, offset).astype(jnp.float32)
        return gated(total)

    def hidden_share_of(name, part):
        def share_of(member):
            return lax.dynamic_slice_in_dim(part, member * share, share, 1)

        total = share_of(group_index).astype(jnp.float32)
        for offset in range(1, group_size):
            with jax.named_scope("terms_" + name):
                moved = over_group(share_of((group_index + offset) % group_size), offset)
                total = total + moved.astype(jnp.float32)
        return gated(total)

    def all_rows(name, piece):
        result = jnp.zeros((piece.shape[0], rows), piece.dtype)
        for offset in range(group_size):
            with jax.named_scope("terms_" + name):
                moved = over_group(piece, offset) if offset else piece
            member = (group_index - offset) % group_size
            result = lax.dynamic_update_slice_in_dim(result, moved, member * share, 1)
        return result

    first = gathered([far], [slab ^ 2, slab ^ 3])
    second = gathered([mid, near], [])
    third = gathered([own], [own, near])

    with jax.named_scope("hop_right1"):
        right1 = over_z(tokens, [(0, 1), (1, 2), (2, 3)])
    with jax.named_scope("hop_left1"):
        left1 = over_z(tokens, [(3, 2), (2, 1), (1, 0)])
    across1 = over_chips("one", first, [])
    across1 = list(hold_until(across1, [right1, left1] + first[-2:] + second + third))

    with jax.named_scope("hop_right2"):
        right2 = over_z(right1, [(1, 2), (2, 3)])
    with jax.named_scope("hop_left2"):
        left2 = over_z(left1, [(2, 1), (1, 0)])
    across2 = over_chips("two", second, across1)
    pieces = over_cores("one", first, across1, merged=False)
    far_in = joined(pieces, 0, rows_in)
    out2 = joined(pieces, rows_in, rows_in + rows_out)
    out3 = joined(pieces, rows_in + rows_out, rows_in + 2 * rows_out)
    with jax.named_scope("hop_edge"):
        edge_in = over_z(far_in, [(0, 1), (3, 2)])

    (out2,) = hold_until([out2], [right2, left2] + across2)
    with jax.named_scope("hop_out2"):
        out2 = over_z(out2, [(a, a ^ 2) for a in range(SLABS)])
    across3 = over_chips("three", third, across2 + [right2, left2])
    pieces = over_cores("two", second, across2)
    mid_in, near_in = joined(pieces, 0, rows_in), joined(pieces, rows_in, 2 * rows_in)
    toward1 = jnp.where(low_half, left1, right1)
    away1 = jnp.where(low_half, right1, left1)
    toward2 = jnp.where(low_half, left2, right2)
    far_hidden = hidden_share_of("far", terms_of(toward2, far_in))
    mid_hidden = hidden_share_of("mid", terms_of(jnp.where(outer, toward2, toward1), mid_in))
    edge_hidden = hidden_share_of("edge", terms_of(toward2, edge_in))
    near_hidden = hidden_of("near", terms_of(jnp.where(outer, toward1, away1), near_in))
    cross_hidden = jnp.where(outer, mid_hidden, far_hidden)
    with jax.named_scope("hop_hidden3"):
        edge_hidden = over_z(edge_hidden, [(1, 3), (2, 0)])

    out3, cross_hidden, mid_hidden = hold_until(
        [out3, cross_hidden, mid_hidden], [out2, near_hidden, edge_hidden]
    )
    across3 = list(hold_until(across3, [out3, cross_hidden, mid_hidden]))
    with jax.named_scope("hop_out3"):
        out3 = over_z(out3, [(a, a ^ 3) for a in range(SLABS)])
    with jax.named_scope("hop_hidden2"):
        hidden2 = over_z(cross_hidden, [(a, a ^ 2) for a in range(SLABS)])
    with jax.named_scope("hop_hidden3"):
        hidden3 = jnp.where(outer, edge_hidden, over_z(mid_hidden, middle))
    pieces = over_cores("three", third, across3)
    own_in = joined(pieces, 0, rows_in)
    out0 = joined(pieces, rows_in, rows_in + rows_out)
    out1 = joined(pieces, rows_in + rows_out, rows_in + 2 * rows_out)
    both1 = jnp.concatenate([out1, near_hidden], axis=1)
    with jax.named_scope("hop_out1"):
        both1 = over_z(both1, [(a, a ^ 1) for a in range(SLABS)])
    out1, hidden1 = both1[:, : out1.shape[1]], both1[:, out1.shape[1] :]
    own_hidden = hidden_of("own", terms_of(tokens, own_in))

    own_pattern = lax.dynamic_index_in_dim(block_pattern, dp_index, 0, keepdims=False)
    scale = route_weight.T * jnp.repeat(own_pattern, block_rows, axis=1).astype(jnp.float32)

    def weighted(hiddens):
        hidden = jnp.concatenate(hiddens, axis=0).astype(jnp.float32)
        hidden = hidden.reshape(-1, slots, units, rows) * scale[None, :, None, :]
        return hidden.astype(jnp.bfloat16).reshape(-1, rows)

    total = lax.dot_general(
        weighted([own_hidden, hidden1]),
        jnp.concatenate([out0, out1], axis=0),
        (((0,), (0,)), ((), ())),
        preferred_element_type=jnp.float32,
    )

    crossed = jnp.concatenate([hidden2, hidden3], axis=0)
    (crossed,) = hold_until([crossed], [out3, own_hidden])
    crossed = weighted([all_rows("rows", crossed)]).T
    return add_product(crossed, out2, out3, total)


def solution(mesh):
    return jax.shard_map(
        on_device,
        mesh=mesh,
        in_specs=(
            P("dp", "group"),
            P(None, "dp", None, "group"),
            P(None, "dp", "group"),
            P(),
            P(),
            P("dp", None),
        ),
        out_specs=P("dp", "group"),
        check_vma=False,
    )
```

```python
import functools

import jax
import jax.numpy as jnp
from jax import lax
from jax.experimental import pallas as pl
from jax.experimental.pallas import tpu as pltpu
from jax.sharding import PartitionSpec as P

SLABS = 4
CORES = 2


def gather_kernel(counts, chosen, proj_in, proj_out, *rest):
    outs, (held_in, flat_in, held_out, sems) = rest[:-4], rest[-4:]
    count_in, count_out = counts
    high_in, high_out = flat_in.shape[1], held_out.shape[1]
    size = count_in * high_in + count_out * high_out
    moves = []
    for core in range(CORES):
        out, base = (outs[0], core * size) if len(outs) == 1 else (outs[core], 0)
        for n in range(count_in + count_out):
            item = core * (count_in + count_out) + n
            if n < count_in:
                slot, row = core * count_in + n, base + n * high_in
                into = pltpu.make_async_copy(
                    proj_in.at[chosen[item]], held_in.at[slot], sems.at[0, item]
                )
                move = pltpu.make_async_copy(
                    flat_in.at[slot], out.at[pl.ds(row, high_in)], sems.at[1, item]
                )
            else:
                slot = core * count_out + n - count_in
                row = base + count_in * high_in + (n - count_in) * high_out
                into = pltpu.make_async_copy(
                    proj_out.at[chosen[item]], held_out.at[slot], sems.at[0, item]
                )
                move = pltpu.make_async_copy(
                    held_out.at[slot], out.at[pl.ds(row, high_out)], sems.at[1, item]
                )
            moves.append((into, move, slot if n < count_in else None))
    for into, _, _ in moves:
        into.start()
    for into, move, slot in moves:
        into.wait()
        if slot is not None:

            @pl.loop(0, high_in // 16)
            def _(block):
                pairs = held_in[slot, pl.ds(block * 8, 8)]
                flat_in[slot, pl.ds(pl.multiple_of(block * 16, 16), 16)] = pairs.reshape(
                    16, flat_in.shape[2]
                )

        move.start()
    for _, move, _ in moves:
        move.wait()


def gather_experts(chosen, proj_in, proj_out, counts, parts):
    width = proj_in.shape[-1]
    high_in, high_out = 2 * proj_in.shape[1], proj_out.shape[1]
    rows = CORES * (counts[0] * high_in + counts[1] * high_out)
    anywhere = pl.BlockSpec(memory_space=pl.ANY)
    got = pl.pallas_call(
        functools.partial(gather_kernel, counts),
        out_shape=[jax.ShapeDtypeStruct((rows // parts, width), proj_in.dtype)] * parts,
        grid_spec=pltpu.PrefetchScalarGridSpec(
            num_scalar_prefetch=1,
            grid=(),
            in_specs=[anywhere] * 2,
            out_specs=[anywhere] * parts,
            scratch_shapes=[
                pltpu.VMEM((max(CORES * counts[0], 1),) + proj_in.shape[1:], proj_in.dtype),
                pltpu.VMEM((max(CORES * counts[0], 1), high_in, width), proj_in.dtype),
                pltpu.VMEM((max(CORES * counts[1], 1), high_out, width), proj_out.dtype),
                pltpu.SemaphoreType.DMA((2, CORES * sum(counts))),
            ],
        ),
        compiler_params=pltpu.CompilerParams(vmem_limit_bytes=40 << 20),
    )(chosen, proj_in, proj_out)
    return list(got)


def hold_kernel(*refs):
    del refs


def hold_until(values, landed):
    count = len(values)
    anywhere = pl.BlockSpec(memory_space=pl.ANY)
    return pl.pallas_call(
        hold_kernel,
        out_shape=[jax.ShapeDtypeStruct(v.shape, v.dtype) for v in values],
        in_specs=[anywhere] * (count + len(landed)),
        out_specs=[anywhere] * count,
        input_output_aliases={n: n for n in range(count)},
        compiler_params=pltpu.CompilerParams(vmem_limit_bytes=1 << 20),
    )(*values, *landed)


def add_product_kernel(left, right_a, right_b, total, result):
    depth = right_a.shape[0]
    product = jnp.dot(left[:, :depth], right_a[...], preferred_element_type=jnp.float32)
    product += jnp.dot(left[:, depth:], right_b[...], preferred_element_type=jnp.float32)
    result[...] = (total[...] + product).astype(result.dtype)


def add_product(left, right_a, right_b, total):
    rows, depth = left.shape
    width = right_a.shape[1]
    block = next(n for n in (512, 384, 256, 128) if width % n == 0)
    return pl.pallas_call(
        add_product_kernel,
        grid=(width // block,),
        in_specs=[
            pl.BlockSpec((rows, depth), lambda n: (0, 0)),
            pl.BlockSpec((depth // 2, block), lambda n: (0, n)),
            pl.BlockSpec((depth // 2, block), lambda n: (0, n)),
            pl.BlockSpec((rows, block), lambda n: (0, n)),
        ],
        out_specs=pl.BlockSpec((rows, block), lambda n: (0, n)),
        out_shape=jax.ShapeDtypeStruct((rows, width), left.dtype),
        compiler_params=pltpu.CompilerParams(vmem_limit_bytes=24 << 20),
    )(left, right_a, right_b, total)


def on_device(tokens, proj_in, proj_out, expert_list, block_pattern, route_weight):
    dp_size = lax.axis_size("dp")
    group_size = lax.axis_size("group")
    peers = dp_size // SLABS
    dp_index = lax.axis_index("dp")
    group_index = lax.axis_index("group")
    slab = dp_index // peers
    column = dp_index % peers
    rows = tokens.shape[0]
    slots = expert_list.shape[1]
    units = proj_in.shape[1]
    block_rows = rows // block_pattern.shape[2]
    share = rows // group_size

    def over_z(value, hops, offset=0):
        pairs = [(a * peers + j, b * peers + (j ^ offset)) for a, b in hops for j in range(peers)]
        return lax.ppermute(value, "dp", pairs)

    def over_group(value, offset):
        pairs = [(g, (g + offset) % group_size) for g in range(group_size)]
        return lax.ppermute(value, "group", pairs)

    same = [(a, a) for a in range(SLABS)]
    middle = [(1, 2), (2, 1)]
    low_half = slab < 2
    outer = (slab == 0) | (slab == 3)
    far, mid, near, own = jnp.where(low_half, 3, 0), jnp.where(low_half, 2, 1), slab ^ 1, slab

    def gathered(in_slabs, out_slabs):
        counts = (slots * len(in_slabs), slots * len(out_slabs))

        def slices(chip, parts):
            chosen = jnp.concatenate(
                [
                    lax.dynamic_index_in_dim(
                        expert_list, s * peers + (column ^ (CORES * chip + core)), 0, keepdims=False
                    )
                    for core in range(CORES)
                    for s in in_slabs + out_slabs
                ]
            )
            return gather_experts(chosen, proj_in, proj_out, counts, parts)

        kept, sibling = slices(0, CORES)
        return [slices(chip, 1)[0] for chip in range(1, peers // CORES)] + [kept, sibling]

    def over_chips(name, gather, start_after):
        sends = gather[:-2]
        if start_after:
            sends = hold_until(sends, start_after)
        with jax.named_scope("hop_chips_" + name):
            return [over_z(v, same, CORES * (n + 1)) for n, v in enumerate(sends)]

    def over_cores(name, gather, across, merged=True):
        kept, sibling = gather[-2:]
        size = kept.shape[0]
        parts = [sibling] + [v[size:] for v in across]
        if merged:
            parts = [jnp.concatenate(parts, axis=0)]
        else:
            parts[:1] = hold_until(parts[:1], across)
        with jax.named_scope("hop_cores_" + name):
            swapped = [over_z(v, same, 1) for v in parts]
        if merged:
            swapped = [swapped[0][n * size : (n + 1) * size] for n in range(1 + len(across))]
        return [kept] + [v[:size] for v in across] + swapped

    def joined(pieces, low, high):
        return jnp.concatenate([v[low:high] for v in pieces], axis=0)

    rows_in, rows_out = slots * units * 2, slots * units

    def terms_of(token_rows, weight_in):
        return lax.dot_general(
            weight_in, token_rows, (((1,), (1,)), ((), ())), preferred_element_type=jnp.float32
        ).astype(jnp.bfloat16)

    def gated(total):
        total = total.reshape(-1, 2, total.shape[1])
        return (jax.nn.silu(total[:, 0]) * total[:, 1]).astype(jnp.bfloat16)

    def hidden_of(name, part):
        total = part.astype(jnp.float32)
        for offset in range(1, group_size):
            with jax.named_scope("terms_" + name):
                total = total + over_group(part, offset).astype(jnp.float32)
        return gated(total)

    def hidden_share_of(name, part):
        def share_of(member):
            return lax.dynamic_slice_in_dim(part, member * share, share, 1)

        total = share_of(group_index).astype(jnp.float32)
        for offset in range(1, group_size):
            with jax.named_scope("terms_" + name):
                moved = over_group(share_of((group_index + offset) % group_size), offset)
                total = total + moved.astype(jnp.float32)
        return gated(total)

    def all_rows(name, piece):
        result = jnp.zeros((piece.shape[0], rows), piece.dtype)
        for offset in range(group_size):
            with jax.named_scope("terms_" + name):
                moved = over_group(piece, offset) if offset else piece
            member = (group_index - offset) % group_size
            result = lax.dynamic_update_slice_in_dim(result, moved, member * share, 1)
        return result

    first = gathered([far], [slab ^ 2, slab ^ 3])
    second = gathered([mid, near], [])
    third = gathered([own], [own, near])

    with jax.named_scope("hop_right1"):
        right1 = over_z(tokens, [(0, 1), (1, 2), (2, 3)])
    with jax.named_scope("hop_left1"):
        left1 = over_z(tokens, [(3, 2), (2, 1), (1, 0)])
    across1 = over_chips("one", first, [])
    across1 = list(hold_until(across1, [right1, left1] + first[-2:] + second + third))

    with jax.named_scope("hop_right2"):
        right2 = over_z(right1, [(1, 2), (2, 3)])
    with jax.named_scope("hop_left2"):
        left2 = over_z(left1, [(2, 1), (1, 0)])
    across2 = over_chips("two", second, across1)
    pieces = over_cores("one", first, across1, merged=False)
    far_in = joined(pieces, 0, rows_in)
    out2 = joined(pieces, rows_in, rows_in + rows_out)
    out3 = joined(pieces, rows_in + rows_out, rows_in + 2 * rows_out)
    with jax.named_scope("hop_edge"):
        edge_in = over_z(far_in, [(0, 1), (3, 2)])

    out2, *across2 = hold_until([out2] + across2, [right2, left2])
    with jax.named_scope("hop_out2"):
        out2 = over_z(out2, [(a, a ^ 2) for a in range(SLABS)])
    across3 = over_chips("three", third, across2 + [right2, left2])
    pieces = over_cores("two", second, across2)
    mid_in, near_in = joined(pieces, 0, rows_in), joined(pieces, rows_in, 2 * rows_in)
    toward1 = jnp.where(low_half, left1, right1)
    away1 = jnp.where(low_half, right1, left1)
    toward2 = jnp.where(low_half, left2, right2)
    far_hidden = hidden_share_of("far", terms_of(toward2, far_in))
    mid_hidden = hidden_share_of("mid", terms_of(jnp.where(outer, toward2, toward1), mid_in))
    edge_hidden = hidden_share_of("edge", terms_of(toward2, edge_in))
    near_hidden = hidden_of("near", terms_of(jnp.where(outer, toward1, away1), near_in))
    cross_hidden = jnp.where(outer, mid_hidden, far_hidden)
    with jax.named_scope("hop_hidden3"):
        edge_hidden = over_z(edge_hidden, [(1, 3), (2, 0)])

    out3, cross_hidden, mid_hidden = hold_until(
        [out3, cross_hidden, mid_hidden], [out2, near_hidden, edge_hidden]
    )
    across3 = list(hold_until(across3, [out3, cross_hidden, mid_hidden]))
    with jax.named_scope("hop_out3"):
        out3 = over_z(out3, [(a, a ^ 3) for a in range(SLABS)])
    with jax.named_scope("hop_hidden2"):
        hidden2 = over_z(cross_hidden, [(a, a ^ 2) for a in range(SLABS)])
    with jax.named_scope("hop_hidden3"):
        hidden3 = jnp.where(outer, edge_hidden, over_z(mid_hidden, middle))
    pieces = over_cores("three", third, across3)
    own_in = joined(pieces, 0, rows_in)
    out0 = joined(pieces, rows_in, rows_in + rows_out)
    out1 = joined(pieces, rows_in + rows_out, rows_in + 2 * rows_out)
    both1 = jnp.concatenate([out1, near_hidden], axis=1)
    with jax.named_scope("hop_out1"):
        both1 = over_z(both1, [(a, a ^ 1) for a in range(SLABS)])
    out1, hidden1 = both1[:, : out1.shape[1]], both1[:, out1.shape[1] :]
    own_hidden = hidden_of("own", terms_of(tokens, own_in))

    own_pattern = lax.dynamic_index_in_dim(block_pattern, dp_index, 0, keepdims=False)
    scale = route_weight.T * jnp.repeat(own_pattern, block_rows, axis=1).astype(jnp.float32)

    def weighted(hiddens):
        hidden = jnp.concatenate(hiddens, axis=0).astype(jnp.float32)
        hidden = hidden.reshape(-1, slots, units, rows) * scale[None, :, None, :]
        return hidden.astype(jnp.bfloat16).reshape(-1, rows)

    total = lax.dot_general(
        weighted([own_hidden, hidden1]),
        jnp.concatenate([out0, out1], axis=0),
        (((0,), (0,)), ((), ())),
        preferred_element_type=jnp.float32,
    )

    crossed = jnp.concatenate([hidden2, hidden3], axis=0)
    (crossed,) = hold_until([crossed], [out3, own_hidden])
    crossed = weighted([all_rows("rows", crossed)]).T
    return add_product(crossed, out2, out3, total)


def solution(mesh):
    return jax.shard_map(
        on_device,
        mesh=mesh,
        in_specs=(
            P("dp", "group"),
            P(None, "dp", None, "group"),
            P(None, "dp", "group"),
            P(),
            P(),
            P("dp", None),
        ),
        out_specs=P("dp", "group"),
        check_vma=False,
    )
```
